1024 devices in a mesh: pipe: 16 (over z_lo, core), expert: 64 (over y, z_hi, x).
Axes of the slice: x: 4, y: 4, z: 32 (z_hi: 4, z_lo: 8; z = z_hi * 8 + z_lo), core: 2. Of those that a mesh axis runs over, the one named last changes fastest.
Arguments:
- forward_rows: bfloat16 [16, 32, 7168], P('pipe', None, 'expert'), may hold values from -6 to 6
- backward_rows: bfloat16 [16, 32, 7168], P('pipe', None, 'expert'), may hold values from -6 to 6
- route_ids: int32 [2, 2, 16, 32, 2], P(None, None, 'pipe'), may hold values from 0 to 3, all different within a row
- norm_gain: float32 [16, 7168], P('pipe'), may hold values from 0.1 to 1.9
- router_weight: float32 [16, 4, 7168], P('pipe'), may hold values from -0.0625 to 0.0625
- w_gate_up: bfloat16 [16, 7168, 8192], P('pipe', None, 'expert'), may hold values from -0.0625 to 0.0625
- w_down: bfloat16 [16, 4096, 7168], P('pipe', None, 'expert'), may hold values from -0.09375 to 0.09375
Outputs:
- forward_out: bfloat16 [16, 32, 7168], P('pipe', None, 'expert')
- backward_out: bfloat16 [16, 32, 7168], P('pipe', None, 'expert')
The draws below stay inside these ranges and needn't reach their ends.
Inputs may be any that keep to these rules, and one draw needn't show every extreme that they name: `route_ids`: each token names 2 different experts.
All inputs are finite; a program needn't handle non-finite values.
Results may differ from the reference program's by a relative error of at most 0.0075.
Values may be sent and summed in bfloat16 or wider, within the bound.
No kernel may reach another device: no remote copies, remote signals or barrier semaphores. Data moves between devices by JAX's collectives and lax.ppermute only.
A program may use at most 32 MiB of HBM per device.

```python
import jax
import jax.numpy as jnp
from jax import lax

D = 7168
FF = 1024
EXPERTS = 4
TOPK = 2
TICKS = 2
MB = 32
SECTIONS = 16
HS = 64
N_EXPERT = 64


def levels(key, dims, cuts, least, high):
    loudness = 1.0
    for axis_at, blocks in cuts:
        steps = jax.random.uniform(jax.random.fold_in(jax.random.fold_in(key, 6), axis_at), (blocks,), jnp.float32, least / len(cuts), high / len(cuts))
        loudness = loudness * jnp.repeat(jnp.exp(steps), dims[axis_at] // blocks).reshape((-1,) + (1,) * (len(dims) - 1 - axis_at))
    return loudness


def different_ones(key, rows, number_of, top, lift):
    sequence = jax.random.permutation(jax.random.fold_in(key, 1), number_of)
    pull = sequence
    for power in range(3):
        pull = pull * pull // number_of
    pull = pull * lift // number_of
    lots = jax.random.randint(jax.random.fold_in(key, 2), (rows, number_of), 0, 4096) + pull
    holders = jax.random.permutation(jax.random.fold_in(key, 3), rows)[jnp.arange(number_of) % rows]
    lots = jnp.where(jnp.arange(rows)[:, None] == holders[None, :], 1 << 14, lots)
    score = lots * number_of + jnp.arange(number_of)
    return lax.top_k(score.astype(jnp.int32), top)[1].astype(jnp.int32)


def noise(key, shape, deviation, bound, shards=(), kind=jnp.bfloat16):
    entries = deviation * jax.random.normal(key, shape, jnp.float32)
    if shards:
        entries = entries * levels(key, shape, shards, -0.22, 0.18)
    return jnp.clip(entries, -bound, bound).astype(kind)


def setup_inputs(seed: int = 0) -> dict:
    seeds = jax.random.split(jax.random.key(seed), 8)
    forward_rows = noise(seeds[0], (SECTIONS, MB, D), 1.0, 6.0, ((0, 16), (2, 64)))
    backward_rows = noise(seeds[1], (SECTIONS, MB, D), 1.0, 6.0, ((0, 16), (2, 64)))
    route_ids = different_ones(seeds[2], TICKS * 2 * SECTIONS * MB, EXPERTS, TOPK, 4096).reshape((TICKS, 2, SECTIONS, MB, TOPK))
    norm_gain = jnp.clip(1.0 + 0.18 * jax.random.normal(seeds[3], (SECTIONS, D), jnp.float32), 0.1, 1.9)
    router_weight = noise(seeds[4], (SECTIONS, EXPERTS, D), D ** -0.5, 0.0625, ((0, 16),), jnp.float32)
    w_gate_up = noise(seeds[5], (SECTIONS, D, 2 * EXPERTS * FF), D ** -0.5, 0.0625, ((0, 16), (2, 64)))
    w_down = noise(seeds[6], (SECTIONS, EXPERTS * FF, D), (EXPERTS * FF) ** -0.5, 0.09375, ((0, 16), (2, 64)))
    return {"forward_rows": forward_rows, "backward_rows": backward_rows, "route_ids": route_ids, "norm_gain": norm_gain, "router_weight": router_weight, "w_gate_up": w_gate_up, "w_down": w_down}


EPSILON = 1e-06
ROUTE_SCALE = 2.5

def section_layer(residual, chosen_ids, gain_row, router_mat, packed_in, down_mat):
    widened = residual.astype(jnp.float32)
    mean_square = lax.optimization_barrier(jnp.mean(widened * widened, axis=-1, keepdims=True))
    normed = (widened * lax.rsqrt(mean_square + EPSILON) * gain_row).astype(jnp.bfloat16)
    logits = lax.dot_general(normed.astype(jnp.float32), router_mat, (((1,), (1,)), ((), ())), precision=lax.Precision.HIGHEST)
    scores = jax.nn.sigmoid(logits)
    picked = jnp.take_along_axis(scores, chosen_ids, axis=1)
    gate_share = picked / lax.optimization_barrier(jnp.sum(picked, axis=1, keepdims=True))
    chosen = (chosen_ids[:, :, None] == jnp.arange(EXPERTS, dtype=jnp.int32)[None, None, :]).astype(jnp.float32)
    route_weight = ROUTE_SCALE * lax.optimization_barrier(jnp.sum(chosen * gate_share[:, :, None], axis=1))
    blocks = packed_in.reshape(D, N_EXPERT, 2, HS)
    gate_w = blocks[:, :, 0, :].reshape(D, EXPERTS * FF)
    up_w = blocks[:, :, 1, :].reshape(D, EXPERTS * FF)
    gate_part = jnp.dot(normed, gate_w, preferred_element_type=jnp.float32)
    up_part = jnp.dot(normed, up_w, preferred_element_type=jnp.float32)
    unit_weight = jnp.repeat(route_weight, FF, axis=1)
    hidden = (jax.nn.silu(gate_part) * up_part * unit_weight).astype(jnp.bfloat16)
    update = jnp.dot(hidden, down_mat, preferred_element_type=jnp.float32)
    return (widened + update).astype(jnp.bfloat16)

def reference(forward_rows, backward_rows, route_ids, norm_gain, router_weight, w_gate_up, w_down):

    def apply_all(states, ids_now):

        def apply_section(operands):
            return section_layer(*operands)
        return lax.map(apply_section, (states, ids_now, norm_gain, router_weight, w_gate_up, w_down))
    bubble = jnp.zeros((1, MB, D), jnp.bfloat16)
    forward = forward_rows
    backward = backward_rows
    for moment in range(TICKS):
        forward = apply_all(forward, route_ids[moment, 0])
        backward = apply_all(backward, route_ids[moment, 1])
        if moment + 1 < TICKS:
            forward = jnp.concatenate([bubble, forward[:-1]], axis=0)
            backward = jnp.concatenate([backward[1:], bubble], axis=0)
    return (forward, backward)
```

```python
import jax
import jax.numpy as jnp
from jax import lax
from jax.sharding import Mesh, PartitionSpec as P

EPSILON = 1e-06
ROUTE_SCALE = 2.5
PLANE = ("y", "x")


def passed_along(block, axis, distance):
    devices = range(lax.axis_size(axis))
    route = [(i - distance, i) for i in devices if i - distance in devices]
    return lax.ppermute(block, axis, route)


def everyone(block, axes):
    size = lax.axis_size(axes)
    return lax.all_to_all(jnp.broadcast_to(block[None], (size, *block.shape)), axes, 0, 0)


def gathered(tile):
    full = everyone(everyone(tile, "zh"), PLANE)
    return full.reshape(-1, tile.shape[1])


def by_plane(array, rows):
    y, zh, x = (lax.axis_size(a) for a in ("y", "zh", "x"))
    split = array.reshape(y, zh, x, 2, rows // 2, array.shape[1])
    return split.transpose(0, 2, 1, 4, 3, 5).reshape(-1, 2, array.shape[1])


def folded(columns):
    half = columns.shape[0] // 2
    return jnp.concatenate([columns[:half], columns[half:]], axis=1)


def unfolded(tile):
    lanes = tile.shape[1] // 2
    return jnp.concatenate([tile[:, :lanes], tile[:, lanes:]], axis=0)


def diagonal(product, rows, lanes):
    return product[:rows, :lanes] + product[rows:, lanes:]


def bf16_pieces(value):
    pieces = []
    for _ in range(3):
        piece = lax.reduce_precision(value, 8, 7)
        pieces.append(piece.astype(jnp.bfloat16))
        value = value - piece
    return pieces


def shards(forward_rows, backward_rows, route_ids, norm_gain, router_weight, w_gate_up, w_down):
    packed_in = w_gate_up[0]
    down_mat = w_down[0]
    share = forward_rows.shape[2]
    batch = forward_rows.shape[1]
    tokens = 2 * batch
    width = packed_in.shape[0]
    columns = packed_in.shape[1]
    units = columns // 2
    experts = router_weight.shape[1]
    steps_total = route_ids.shape[0]
    own_expert = lax.axis_index(("y", "zh", "x")) * units // (down_mat.shape[0] // experts)

    gain = norm_gain[0][:, None]
    scaled_in = (packed_in.astype(jnp.float32) * gain).astype(jnp.bfloat16)
    in_t = by_plane(scaled_in, share).reshape(width // 2, 2 * columns).T
    router_cols = by_plane(router_weight[0].T * gain, share)
    router_cols = router_cols.reshape(width // 2, 2 * experts)
    router_t = jnp.concatenate(bf16_pieces(router_cols.T), axis=0)
    in_t = jnp.concatenate([in_t, router_t], axis=0)
    down_t = by_plane(down_mat, units).reshape(down_mat.shape[0] // 2, 2 * share).T

    lane = lax.broadcasted_iota(jnp.int32, (1, 2 * tokens), 1)
    is_forward = lane % tokens < batch
    state = jnp.concatenate([forward_rows[0], backward_rows[0]], axis=0).T
    tile = folded(state)
    for moment in range(steps_total):
        rows = gathered(tile)
        wide = rows.astype(jnp.float32)
        squares = jnp.sum(wide * wide, axis=0, keepdims=True)
        mean_square = (squares[:, :tokens] + squares[:, tokens:]) / width
        inverse = lax.rsqrt(mean_square + EPSILON)
        product = jnp.dot(in_t, rows, preferred_element_type=jnp.float32)
        projected = diagonal(product[: 2 * columns], columns, tokens) * inverse
        routed = product[2 * columns :].reshape(3, 2 * experts, 2 * tokens).sum(0)
        scores = jax.nn.sigmoid(diagonal(routed, experts, tokens) * inverse)
        ids = jnp.concatenate([route_ids[moment, 0, 0], route_ids[moment, 1, 0]], axis=0).T
        named = lax.broadcasted_iota(jnp.int32, (experts, 1), 0)[:, None] == ids[None]
        picked = jnp.sum(jnp.where(named, scores[:, None], 0.0), axis=0)
        total = jnp.sum(picked, axis=0, keepdims=True)
        mine = jnp.sum(jnp.where(ids == own_expert, picked, 0.0), axis=0, keepdims=True)
        weight = ROUTE_SCALE * (mine / total)
        hidden = jax.nn.silu(projected[:units]) * projected[units:] * weight
        everything = gathered(folded(hidden.astype(jnp.bfloat16)))
        update = jnp.dot(down_t, everything, preferred_element_type=jnp.float32)
        state = state.astype(jnp.float32) + diagonal(update, share, tokens)
        state = state.astype(jnp.bfloat16)
        if moment + 1 < steps_total:
            tile = folded(state)
            tile = jnp.where(
                is_forward, passed_along(tile, "pipe", 1), passed_along(tile, "pipe", -1)
            )
            state = unfolded(tile)
    final = state.T
    return (final[None, :batch], final[None, batch:])


def solution(mesh):
    fine = Mesh(mesh.devices.reshape(-1, 4, 4, 4), ("pipe", "y", "zh", "x"))
    expert = ("y", "zh", "x")
    return jax.shard_map(
        shards,
        mesh=fine,
        in_specs=(
            P("pipe", None, expert),
            P("pipe", None, expert),
            P(None, None, "pipe", None, None),
            P("pipe", None),
            P("pipe", None, None),
            P("pipe", None, expert),
            P("pipe", None, expert),
        ),
        out_specs=(P("pipe", None, expert), P("pipe", None, expert)),
        check_vma=False,
    )
```

```python
import jax
import jax.numpy as jnp
from jax import lax
from jax.experimental import pallas as pl
from jax.experimental.pallas import tpu as pltpu
from jax.sharding import Mesh, PartitionSpec as P

EPSILON = 1e-06
ROUTE_SCALE = 2.5
PLANE = ("y", "x")
EXPERT = ("y", "zh", "x")
LANES = 128
STATS = 16


def passed_along(block, axis, distance):
    devices = range(lax.axis_size(axis))
    route = [(i - distance, i) for i in devices if i - distance in devices]
    return lax.ppermute(block, axis, route)


def everyone(copies, axes):
    return lax.all_to_all(copies, axes, 0, 0)


def gathered(copies):
    column = everyone(copies, "zh")
    size = lax.axis_size(PLANE)
    full = everyone(jnp.broadcast_to(column[None], (size, *column.shape)), PLANE)
    return full.reshape(-1, *copies.shape[1:])


def lower_lanes(shape):
    return lax.broadcasted_iota(jnp.int32, shape, 1) < LANES // 2


def turned(value):
    return pltpu.roll(value, LANES // 2, 1)


def natural(place, sizes):
    y, zh, x = sizes
    at_y, rest = divmod(place, x * zh)
    at_x, at_zh = divmod(rest, zh)
    return (at_y * zh + at_zh) * x + at_x


def write_tile(rows, coefs, tile_ref):
    scaled = rows * coefs[:, 0:1]
    sums = [jnp.sum(rows * rows, axis=0, keepdims=True)]
    for e in range(1, 5):
        sums.append(jnp.sum(rows * coefs[:, e : e + 1], axis=0, keepdims=True))
    sums.append(jnp.zeros((3, LANES), jnp.float32))
    sums = jnp.concatenate(sums, axis=0)
    high = sums.astype(jnp.bfloat16).astype(jnp.float32)
    upper = jnp.concatenate([scaled[64:], high, sums - high], axis=0)
    tile = jnp.where(lower_lanes((64, LANES)), scaled[:64], turned(upper))
    tile = tile.astype(jnp.bfloat16)
    for copy in range(tile_ref.shape[0]):
        tile_ref[copy] = tile


def enter_kernel(forward_ref, backward_ref, coefs_ref, tile_ref, state_ref):
    f = forward_ref[...].astype(jnp.float32)
    b = backward_ref[...].astype(jnp.float32)
    rows = jnp.concatenate([f, b, f, b], axis=0).T
    state_ref[...] = rows
    write_tile(rows, coefs_ref[...], tile_ref)


def pass_kernel(previous_ref, next_ref, coefs_ref, tile_ref, state_ref):
    lane = lax.broadcasted_iota(jnp.int32, (64, LANES), 1)
    mixed = jnp.where(
        lane % 64 < 32,
        previous_ref[...].astype(jnp.float32),
        next_ref[...].astype(jnp.float32),
    )
    rows = jnp.concatenate([mixed, turned(mixed)[:48]], axis=0)
    state_ref[...] = rows
    write_tile(rows, coefs_ref[...], tile_ref)


def hidden_kernel(sizes, width, own_ref, gathered_ref, weight_ref, ids_ref, out_ref, rows_ref):
    share = weight_ref.shape[1] // gathered_ref.shape[0]
    stats = jnp.zeros((STATS, LANES), jnp.float32)
    for place in range(gathered_ref.shape[0]):
        tile = gathered_ref[place].astype(jnp.float32)
        start = natural(place, sizes) * share
        rows_ref[start : start + 64, :] = gathered_ref[place]
        rows_ref[start + 64 : start + share, :] = turned(tile[:48]).astype(jnp.bfloat16)
        stats = stats + tile[48:]
    stats = turned(stats[:8] + stats[8:])
    inverse = lax.rsqrt(stats[0:1] / width + EPSILON)
    projected = jnp.dot(
        weight_ref[...], rows_ref[...], preferred_element_type=jnp.float32
    ) * inverse
    scores = 1.0 / (1.0 + jnp.exp(-(stats[1:5] * inverse)))
    total = jnp.zeros((1, LANES), jnp.float32)
    mine = jnp.zeros((1, LANES), jnp.float32)
    for k in range(ids_ref.shape[0]):
        ids = ids_ref[k : k + 1, :]
        picked = jnp.zeros((1, LANES), jnp.float32)
        for e in range(4):
            picked = jnp.where(ids == e, scores[e : e + 1], picked)
        total = total + picked
        mine = mine + jnp.where(ids == own_ref[0], picked, 0.0)
    weight = ROUTE_SCALE * (mine / total)
    gate, up = projected[:64], projected[64:]
    hidden = gate / (1.0 + jnp.exp(-gate)) * up * weight
    folded = jnp.where(lower_lanes((32, LANES)), hidden[:32], turned(hidden[32:]))
    folded = folded.astype(jnp.bfloat16)
    for copy in range(out_ref.shape[0]):
        out_ref[copy] = folded


def updated(sizes, gathered_ref, weight_ref, state_ref, rows_ref):
    for place in range(gathered_ref.shape[0]):
        start = natural(place, sizes) * 64
        rows_ref[start : start + 32, :] = gathered_ref[place]
        rows_ref[start + 32 : start + 64, :] = turned(
            gathered_ref[place].astype(jnp.float32)
        ).astype(jnp.bfloat16)
    return state_ref[...] + jnp.dot(
        weight_ref[...], rows_ref[...], preferred_element_type=jnp.float32
    )


def middle_kernel(sizes, gathered_ref, weight_ref, state_ref, out_ref, rows_ref):
    state = updated(sizes, gathered_ref, weight_ref, state_ref, rows_ref)
    upper = jnp.concatenate([state[64:], jnp.zeros((16, LANES), jnp.float32)], axis=0)
    tile = jnp.where(lower_lanes((64, LANES)), state[:64], turned(upper))
    out_ref[...] = tile.astype(jnp.bfloat16)


def last_kernel(sizes, gathered_ref, weight_ref, state_ref, forward_ref, backward_ref, rows_ref):
    state = updated(sizes, gathered_ref, weight_ref, state_ref, rows_ref).T
    forward_ref[...] = state[:32].astype(jnp.bfloat16)
    backward_ref[...] = state[32:64].astype(jnp.bfloat16)


def local(kernel, outs, scratch, flops, *args, scalars=0):
    vmem = pl.BlockSpec(memory_space=pltpu.VMEM)
    smem = pl.BlockSpec(memory_space=pltpu.SMEM)
    moved = sum(a.size * a.dtype.itemsize for a in (*args, *outs))
    return pl.pallas_call(
        kernel,
        out_shape=outs,
        in_specs=[smem] * scalars + [vmem] * (len(args) - scalars),
        out_specs=tuple(vmem for _ in outs),
        scratch_shapes=scratch,
        cost_estimate=pl.CostEstimate(flops=flops, bytes_accessed=moved, transcendentals=0),
        compiler_params=pltpu.CompilerParams(vmem_limit_bytes=16 * 2**20),
    )(*args)


def shards(forward_rows, backward_rows, route_ids, norm_gain, router_weight, w_gate_up, w_down):
    sizes = tuple(lax.axis_size(a) for a in EXPERT)
    share = forward_rows.shape[2]
    width, columns = w_gate_up.shape[1:]
    all_units = w_down.shape[1]
    me = lax.axis_index(EXPERT)
    own = (me * (columns // 2) // (all_units // router_weight.shape[1])).reshape(1)
    steps_total = route_ids.shape[0]
    tile = (64, LANES)
    half = jnp.bfloat16

    gain = lax.dynamic_slice_in_dim(norm_gain, me * share, share, 1)
    router = lax.dynamic_slice_in_dim(router_weight[0], me * share, share, 1)
    coefs = jnp.concatenate([gain, router * gain, jnp.zeros((3, share), jnp.float32)], axis=0).T
    both = route_ids[:, :, 0].transpose(0, 3, 1, 2).reshape(steps_total, 2, -1)
    both = jnp.concatenate([both, both], axis=2)

    entry_outs = (
        jax.ShapeDtypeStruct((sizes[1], *tile), half),
        jax.ShapeDtypeStruct((share, LANES), jnp.float32),
    )
    copies, state = local(
        enter_kernel, entry_outs, [], 0, forward_rows[0], backward_rows[0], coefs
    )
    in_t = w_gate_up[0].T
    down_t = w_down[0].T
    for moment in range(steps_total):
        rows = gathered(copies)
        (hidden,) = local(
            lambda *refs: hidden_kernel(sizes, width, *refs),
            (jax.ShapeDtypeStruct((sizes[1], 32, LANES), half),),
            [pltpu.VMEM((width, LANES), half)],
            2 * width * columns * LANES,
            own,
            rows,
            in_t,
            both[moment],
            scalars=1,
        )
        units = gathered(hidden)
        scratch = [pltpu.VMEM((all_units, LANES), half)]
        flops = 2 * all_units * share * LANES
        if moment + 1 < steps_total:
            (raw,) = local(
                lambda *refs: middle_kernel(sizes, *refs),
                (jax.ShapeDtypeStruct(tile, half),),
                scratch,
                flops,
                units,
                down_t,
                state,
            )
            copies, state = local(
                pass_kernel,
                entry_outs,
                [],
                0,
                passed_along(raw, "pipe", 1),
                passed_along(raw, "pipe", -1),
                coefs,
            )
        else:
            rows_out = jax.ShapeDtypeStruct((forward_rows.shape[1], share), half)
            outs = local(
                lambda *refs: last_kernel(sizes, *refs),
                (rows_out, rows_out),
                scratch,
                flops,
                units,
                down_t,
                state,
            )
    return (outs[0][None], outs[1][None])


def solution(mesh):
    fine = Mesh(mesh.devices.reshape(-1, 4, 4, 4), ("pipe", *EXPERT))
    return jax.shard_map(
        shards,
        mesh=fine,
        in_specs=(
            P("pipe", None, EXPERT),
            P("pipe", None, EXPERT),
            P(None, None, "pipe", None, None),
            P("pipe", None),
            P("pipe", None, None),
            P("pipe", None, EXPERT),
            P("pipe", None, EXPERT),
        ),
        out_specs=(P("pipe", None, EXPERT), P("pipe", None, EXPERT)),
        check_vma=False,
    )
```

```python
import jax
import jax.numpy as jnp
from jax import lax
from jax.experimental import pallas as pl
from jax.experimental.pallas import tpu as pltpu
from jax.sharding import Mesh, PartitionSpec as P

EPSILON = 1e-06
ROUTE_SCALE = 2.5
PLANE = ("y", "x")
EXPERT = ("y", "zh", "x")
LANES = 128
STATS = 16
VMEM_MIB = 60


def passed_along(block, axis, distance):
    devices = range(lax.axis_size(axis))
    route = [(i - distance, i) for i in devices if i - distance in devices]
    return lax.ppermute(block, axis, route)


def everyone(copies, axes):
    return lax.all_to_all(copies, axes, 0, 0)


def gathered(copies, meanwhile=()):
    column = everyone(copies, "zh")
    column, meanwhile = lax.optimization_barrier((column, meanwhile))
    size = lax.axis_size(PLANE)
    full = everyone(jnp.broadcast_to(column[None], (size, *column.shape)), PLANE)
    return full.reshape(-1, *copies.shape[1:]), meanwhile


def lower_lanes(shape):
    return lax.broadcasted_iota(jnp.int32, shape, 1) < LANES // 2


def turned(value):
    return pltpu.roll(value, LANES // 2, 1)


def natural(place, sizes):
    y, zh, x = sizes
    at_y, rest = divmod(place, x * zh)
    at_x, at_zh = divmod(rest, zh)
    return (at_y * zh + at_zh) * x + at_x


def write_tile(rows, coefs, tile_ref):
    scaled = rows * coefs[:, 0:1]
    sums = [jnp.sum(rows * rows, axis=0, keepdims=True)]
    for e in range(1, 5):
        sums.append(jnp.sum(rows * coefs[:, e : e + 1], axis=0, keepdims=True))
    sums.append(jnp.zeros((3, LANES), jnp.float32))
    sums = jnp.concatenate(sums, axis=0)
    high = sums.astype(jnp.bfloat16).astype(jnp.float32)
    upper = jnp.concatenate([scaled[64:], high, sums - high], axis=0)
    tile = jnp.where(lower_lanes((64, LANES)), scaled[:64], turned(upper))
    tile = tile.astype(jnp.bfloat16)
    for copy in range(tile_ref.shape[0]):
        tile_ref[copy] = tile


def enter_kernel(
    me_ref,
    forward_hbm,
    backward_hbm,
    gain_hbm,
    router_hbm,
    tile_ref,
    state_ref,
    coefs_ref,
    forward_ref,
    backward_ref,
    gain_ref,
    router_ref,
    arrived,
):
    pairs = (
        (gain_hbm, gain_ref),
        (router_hbm, router_ref),
        (forward_hbm, forward_ref),
        (backward_hbm, backward_ref),
    )
    fetches = [
        pltpu.make_async_copy(source, target, arrived.at[i])
        for i, (source, target) in enumerate(pairs)
    ]
    for fetch in fetches:
        fetch.start()
    for fetch in fetches:
        fetch.wait()
    share = forward_ref.shape[1]
    window = 2 * LANES
    start = me_ref[0] * share
    last = gain_ref.shape[1] // LANES - 2
    base = pl.multiple_of(jnp.minimum(start // LANES, last) * LANES, LANES)
    gain = gain_ref[:, pl.ds(base, window)]
    router = router_ref[:, pl.ds(base, window)]
    coefs = jnp.concatenate(
        [gain, router * gain, jnp.zeros((3, window), jnp.float32)], axis=0
    )
    coefs = pltpu.roll(coefs, lax.rem(window - (start - base), window), 1)
    coefs = coefs[:, :LANES].T[:share]
    coefs_ref[...] = coefs
    f = forward_ref[...].astype(jnp.float32)
    b = backward_ref[...].astype(jnp.float32)
    rows = jnp.concatenate([f, b, f, b], axis=0).T
    state_ref[...] = rows
    write_tile(rows, coefs, tile_ref)


def pass_kernel(previous_ref, next_ref, coefs_ref, tile_ref, state_ref):
    lane = lax.broadcasted_iota(jnp.int32, (64, LANES), 1)
    mixed = jnp.where(
        lane % 64 < 32,
        previous_ref[...].astype(jnp.float32),
        next_ref[...].astype(jnp.float32),
    )
    rows = jnp.concatenate([mixed, turned(mixed)[:48]], axis=0)
    state_ref[...] = rows
    write_tile(rows, coefs_ref[...], tile_ref)


def hidden_kernel(sizes, width, own_ref, gathered_ref, weight_ref, ids_ref, out_ref, rows_ref):
    share = weight_ref.shape[1] // gathered_ref.shape[0]
    stats = jnp.zeros((STATS, LANES), jnp.float32)
    for place in range(gathered_ref.shape[0]):
        tile = gathered_ref[place].astype(jnp.float32)
        start = natural(place, sizes) * share
        rows_ref[start : start + 64, :] = gathered_ref[place]
        rows_ref[start + 64 : start + share, :] = turned(tile[:48]).astype(jnp.bfloat16)
        stats = stats + tile[48:]
    stats = turned(stats[:8] + stats[8:])
    inverse = lax.rsqrt(stats[0:1] / width + EPSILON)
    projected = jnp.dot(
        weight_ref[...], rows_ref[...], preferred_element_type=jnp.float32
    ) * inverse
    scores = 1.0 / (1.0 + jnp.exp(-(stats[1:5] * inverse)))
    total = jnp.zeros((1, LANES), jnp.float32)
    mine = jnp.zeros((1, LANES), jnp.float32)
    for k in range(ids_ref.shape[0]):
        ids = ids_ref[k : k + 1, :]
        picked = jnp.zeros((1, LANES), jnp.float32)
        for e in range(4):
            picked = jnp.where(ids == e, scores[e : e + 1], picked)
        total = total + picked
        mine = mine + jnp.where(ids == own_ref[0], picked, 0.0)
    weight = ROUTE_SCALE * (mine / total)
    gate, up = projected[:64], projected[64:]
    hidden = gate / (1.0 + jnp.exp(-gate)) * up * weight
    folded = jnp.where(lower_lanes((32, LANES)), hidden[:32], turned(hidden[32:]))
    folded = folded.astype(jnp.bfloat16)
    for copy in range(out_ref.shape[0]):
        out_ref[copy] = folded


def updated(sizes, gathered_ref, weight_ref, state_ref, rows_ref):
    for place in range(gathered_ref.shape[0]):
        start = natural(place, sizes) * 64
        rows_ref[start : start + 32, :] = gathered_ref[place]
        rows_ref[start + 32 : start + 64, :] = turned(
            gathered_ref[place].astype(jnp.float32)
        ).astype(jnp.bfloat16)
    return state_ref[...] + jnp.dot(
        weight_ref[...], rows_ref[...], preferred_element_type=jnp.float32
    )


def middle_kernel(sizes, gathered_ref, weight_ref, state_ref, out_ref, rows_ref):
    state = updated(sizes, gathered_ref, weight_ref, state_ref, rows_ref)
    upper = jnp.concatenate([state[64:], jnp.zeros((16, LANES), jnp.float32)], axis=0)
    tile = jnp.where(lower_lanes((64, LANES)), state[:64], turned(upper))
    out_ref[...] = tile.astype(jnp.bfloat16)


def last_kernel(sizes, gathered_ref, weight_ref, state_ref, forward_ref, backward_ref, rows_ref):
    state = updated(sizes, gathered_ref, weight_ref, state_ref, rows_ref).T
    forward_ref[...] = state[:32].astype(jnp.bfloat16)
    backward_ref[...] = state[32:64].astype(jnp.bfloat16)


def local(kernel, outs, scratch, flops, *args, scalars=0, space=pltpu.VMEM, vmem=16):
    onchip = pl.BlockSpec(memory_space=pltpu.VMEM)
    given = pl.BlockSpec(memory_space=space)
    smem = pl.BlockSpec(memory_space=pltpu.SMEM)
    moved = sum(a.size * a.dtype.itemsize for a in (*args, *outs))
    return pl.pallas_call(
        kernel,
        out_shape=outs,
        in_specs=[smem] * scalars + [given] * (len(args) - scalars),
        out_specs=tuple(onchip for _ in outs),
        scratch_shapes=scratch,
        cost_estimate=pl.CostEstimate(flops=flops, bytes_accessed=moved, transcendentals=0),
        compiler_params=pltpu.CompilerParams(vmem_limit_bytes=vmem * 2**20),
    )(*args)


def shards(forward_rows, backward_rows, route_ids, norm_gain, router_weight, w_gate_up, w_down):
    sizes = tuple(lax.axis_size(a) for a in EXPERT)
    share = forward_rows.shape[2]
    width, columns = w_gate_up.shape[1:]
    all_units = w_down.shape[1]
    me = lax.axis_index(EXPERT)
    own = (me * (columns // 2) // (all_units // router_weight.shape[1])).reshape(1)
    steps_total = route_ids.shape[0]
    tile = (64, LANES)
    half = jnp.bfloat16

    entry_outs = (
        jax.ShapeDtypeStruct((sizes[1], *tile), half),
        jax.ShapeDtypeStruct((share, LANES), jnp.float32),
    )
    copies, state, coefs = local(
        enter_kernel,
        (*entry_outs, jax.ShapeDtypeStruct((share, 8), jnp.float32)),
        [
            pltpu.VMEM(forward_rows.shape[1:], half),
            pltpu.VMEM(backward_rows.shape[1:], half),
            pltpu.VMEM(norm_gain.shape, jnp.float32),
            pltpu.VMEM(router_weight.shape[1:], jnp.float32),
            pltpu.SemaphoreType.DMA((4,)),
        ],
        0,
        me.reshape(1),
        forward_rows[0],
        backward_rows[0],
        norm_gain,
        router_weight[0],
        scalars=1,
        space=pltpu.HBM,
        vmem=VMEM_MIB,
    )
    copies, packed_in, route_ids = lax.optimization_barrier((copies, w_gate_up, route_ids))
    in_t = packed_in[0].T
    both = route_ids[:, :, 0].transpose(0, 3, 1, 2).reshape(steps_total, 2, -1)
    both = jnp.concatenate([both, both], axis=2)
    down_t = w_down[0].T
    for moment in range(steps_total):
        rows, (in_t, both) = gathered(copies, (in_t, both))
        (hidden,) = local(
            lambda *refs: hidden_kernel(sizes, width, *refs),
            (jax.ShapeDtypeStruct((sizes[1], 32, LANES), half),),
            [pltpu.VMEM((width, LANES), half)],
            2 * width * columns * LANES,
            own,
            rows,
            in_t,
            both[moment],
            scalars=1,
        )
        units, _ = gathered(hidden)
        scratch = [pltpu.VMEM((all_units, LANES), half)]
        flops = 2 * all_units * share * LANES
        if moment + 1 < steps_total:
            (raw,) = local(
                lambda *refs: middle_kernel(sizes, *refs),
                (jax.ShapeDtypeStruct(tile, half),),
                scratch,
                flops,
                units,
                down_t,
                state,
            )
            copies, state = local(
                pass_kernel,
                entry_outs,
                [],
                0,
                passed_along(raw, "pipe", 1),
                passed_along(raw, "pipe", -1),
                coefs,
            )
        else:
            rows_out = jax.ShapeDtypeStruct((forward_rows.shape[1], share), half)
            outs = local(
                lambda *refs: last_kernel(sizes, *refs),
                (rows_out, rows_out),
                scratch,
                flops,
                units,
                down_t,
                state,
            )
    return (outs[0][None], outs[1][None])


def solution(mesh):
    fine = Mesh(mesh.devices.reshape(-1, 4, 4, 4), ("pipe", *EXPERT))
    return jax.shard_map(
        shards,
        mesh=fine,
        in_specs=(
            P("pipe", None, EXPERT),
            P("pipe", None, EXPERT),
            P(None, None, "pipe", None, None),
            P("pipe", None),
            P("pipe", None, None),
            P("pipe", None, EXPERT),
            P("pipe", None, EXPERT),
        ),
        out_specs=(P("pipe", None, EXPERT), P("pipe", None, EXPERT)),
        check_vma=False,
    )
```

```python
import jax
import jax.numpy as jnp
from jax import lax
from jax.experimental import pallas as pl
from jax.experimental.pallas import tpu as pltpu
from jax.sharding import Mesh, PartitionSpec as P

EPSILON = 1e-06
ROUTE_SCALE = 2.5
PLANE = ("y", "x")
EXPERT = ("y", "zh", "x")
LANES = 128
STATS = 16


def passed_along(block, axis, distance):
    devices = range(lax.axis_size(axis))
    route = [(i - distance, i) for i in devices if i - distance in devices]
    return lax.ppermute(block, axis, route)


def everyone(copies, axes):
    return lax.all_to_all(copies, axes, 0, 0)


def gathered(copies):
    column = everyone(copies, "zh")
    size = lax.axis_size(PLANE)
    full = everyone(jnp.broadcast_to(column[None], (size, *column.shape)), PLANE)
    return full.reshape(-1, *copies.shape[1:])


def lower_lanes(shape):
    return lax.broadcasted_iota(jnp.int32, shape, 1) < LANES // 2


def turned(value):
    return pltpu.roll(value, LANES // 2, 1)


def natural(place, sizes):
    y, zh, x = sizes
    at_y, rest = divmod(place, x * zh)
    at_x, at_zh = divmod(rest, zh)
    return (at_y * zh + at_zh) * x + at_x


def write_tile(rows, coefs, tile_ref):
    scaled = rows * coefs[:, 0:1]
    sums = [jnp.sum(rows * rows, axis=0, keepdims=True)]
    for e in range(1, 5):
        sums.append(jnp.sum(rows * coefs[:, e : e + 1], axis=0, keepdims=True))
    sums.append(jnp.zeros((3, LANES), jnp.float32))
    sums = jnp.concatenate(sums, axis=0)
    high = sums.astype(jnp.bfloat16).astype(jnp.float32)
    upper = jnp.concatenate([scaled[64:], high, sums - high], axis=0)
    tile = jnp.where(lower_lanes((64, LANES)), scaled[:64], turned(upper))
    tile = tile.astype(jnp.bfloat16)
    for copy in range(tile_ref.shape[0]):
        tile_ref[copy] = tile


def enter_kernel(
    me_ref,
    forward_hbm,
    backward_hbm,
    gain_hbm,
    router_hbm,
    tile_ref,
    state_ref,
    coefs_ref,
    forward_ref,
    backward_ref,
    gain_ref,
    router_ref,
    arrived,
):
    pairs = (
        (gain_hbm, gain_ref),
        (router_hbm, router_ref),
        (forward_hbm, forward_ref),
        (backward_hbm, backward_ref),
    )
    fetches = [
        pltpu.make_async_copy(source, target, arrived.at[i])
        for i, (source, target) in enumerate(pairs)
    ]
    for fetch in fetches:
        fetch.start()
    for fetch in fetches:
        fetch.wait()
    share = forward_ref.shape[1]
    window = 2 * LANES
    start = me_ref[0] * share
    last = gain_ref.shape[1] // LANES - 2
    base = pl.multiple_of(jnp.minimum(start // LANES, last) * LANES, LANES)
    gain = gain_ref[:, pl.ds(base, window)]
    router = router_ref[:, pl.ds(base, window)]
    coefs = jnp.concatenate(
        [gain, router * gain, jnp.zeros((3, window), jnp.float32)], axis=0
    )
    coefs = pltpu.roll(coefs, lax.rem(window - (start - base), window), 1)
    coefs = coefs[:, :LANES].T[:share]
    coefs_ref[...] = coefs
    f = forward_ref[...].astype(jnp.float32)
    b = backward_ref[...].astype(jnp.float32)
    rows = jnp.concatenate([f, b, f, b], axis=0).T
    state_ref[...] = rows
    write_tile(rows, coefs, tile_ref)


def pass_kernel(previous_ref, next_ref, coefs_ref, tile_ref, state_ref):
    lane = lax.broadcasted_iota(jnp.int32, (64, LANES), 1)
    mixed = jnp.where(
        lane % 64 < 32,
        previous_ref[...].astype(jnp.float32),
        next_ref[...].astype(jnp.float32),
    )
    rows = jnp.concatenate([mixed, turned(mixed)[:48]], axis=0)
    state_ref[...] = rows
    write_tile(rows, coefs_ref[...], tile_ref)


def hidden_kernel(
    sizes, moment, sharers, me_ref, gathered_ref, weight_ref, ids_ref, out_ref, rows_ref
):
    width = weight_ref.shape[0]
    share = weight_ref.shape[0] // gathered_ref.shape[0]
    stats = jnp.zeros((STATS, LANES), jnp.float32)
    for place in range(gathered_ref.shape[0]):
        tile = gathered_ref[place].astype(jnp.float32)
        start = natural(place, sizes) * share
        rows_ref[start : start + 64, :] = gathered_ref[place]
        rows_ref[start + 64 : start + share, :] = turned(tile[:48]).astype(jnp.bfloat16)
        stats = stats + tile[48:]
    stats = turned(stats[:8] + stats[8:])
    inverse = lax.rsqrt(stats[0:1] / width + EPSILON)
    projected = lax.dot_general(
        weight_ref[...],
        rows_ref[...],
        (((0,), (0,)), ((), ())),
        preferred_element_type=jnp.float32,
    ) * inverse
    scores = 1.0 / (1.0 + jnp.exp(-(stats[1:5] * inverse)))
    own = lax.div(me_ref[0], sharers)
    chosen = jnp.concatenate([ids_ref[moment, 0], ids_ref[moment, 1]] * 2, axis=1)
    total = jnp.zeros((1, LANES), jnp.float32)
    mine = jnp.zeros((1, LANES), jnp.float32)
    for k in range(chosen.shape[0]):
        ids = chosen[k : k + 1]
        picked = jnp.zeros((1, LANES), jnp.float32)
        for e in range(4):
            picked = jnp.where(ids == e, scores[e : e + 1], picked)
        total = total + picked
        mine = mine + jnp.where(ids == own, picked, 0.0)
    weight = ROUTE_SCALE * (mine / total)
    gate, up = projected[:64], projected[64:]
    hidden = gate / (1.0 + jnp.exp(-gate)) * up * weight
    folded = jnp.where(lower_lanes((32, LANES)), hidden[:32], turned(hidden[32:]))
    folded = folded.astype(jnp.bfloat16)
    for copy in range(out_ref.shape[0]):
        out_ref[copy] = folded


def updated(sizes, gathered_ref, weight_ref, state_ref, rows_ref):
    for place in range(gathered_ref.shape[0]):
        start = natural(place, sizes) * 64
        rows_ref[start : start + 32, :] = gathered_ref[place]
        rows_ref[start + 32 : start + 64, :] = turned(
            gathered_ref[place].astype(jnp.float32)
        ).astype(jnp.bfloat16)
    return state_ref[...] + jnp.dot(
        weight_ref[...], rows_ref[...], preferred_element_type=jnp.float32
    )


def middle_kernel(sizes, gathered_ref, weight_ref, state_ref, out_ref, rows_ref):
    state = updated(sizes, gathered_ref, weight_ref, state_ref, rows_ref)
    upper = jnp.concatenate([state[64:], jnp.zeros((16, LANES), jnp.float32)], axis=0)
    tile = jnp.where(lower_lanes((64, LANES)), state[:64], turned(upper))
    out_ref[...] = tile.astype(jnp.bfloat16)


def last_kernel(sizes, gathered_ref, weight_ref, state_ref, forward_ref, backward_ref, rows_ref):
    state = updated(sizes, gathered_ref, weight_ref, state_ref, rows_ref).T
    forward_ref[...] = state[:32].astype(jnp.bfloat16)
    backward_ref[...] = state[32:64].astype(jnp.bfloat16)


def local(kernel, outs, scratch, flops, *args, scalars=0, space=pltpu.VMEM, vmem=16):
    onchip = pl.BlockSpec(memory_space=pltpu.VMEM)
    given = pl.BlockSpec(memory_space=space)
    smem = pl.BlockSpec(memory_space=pltpu.SMEM)
    moved = sum(a.size * a.dtype.itemsize for a in (*args, *outs))
    return pl.pallas_call(
        kernel,
        out_shape=outs,
        in_specs=[smem] * scalars + [given] * (len(args) - scalars),
        out_specs=tuple(onchip for _ in outs),
        scratch_shapes=scratch,
        cost_estimate=pl.CostEstimate(flops=flops, bytes_accessed=moved, transcendentals=0),
        compiler_params=pltpu.CompilerParams(vmem_limit_bytes=vmem * 2**20),
    )(*args)


def shards(forward_rows, backward_rows, route_ids, norm_gain, router_weight, w_gate_up, w_down):
    sizes = tuple(lax.axis_size(a) for a in EXPERT)
    share = forward_rows.shape[2]
    width, columns = w_gate_up.shape[1:]
    all_units = w_down.shape[1]
    me = lax.axis_index(EXPERT).reshape(1)
    sharers = all_units // router_weight.shape[1] // (columns // 2)
    steps_total = route_ids.shape[0]
    tile = (64, LANES)
    half = jnp.bfloat16

    entry_outs = (
        jax.ShapeDtypeStruct((sizes[1], *tile), half),
        jax.ShapeDtypeStruct((share, LANES), jnp.float32),
    )
    copies, state, coefs = local(
        enter_kernel,
        (*entry_outs, jax.ShapeDtypeStruct((share, 8), jnp.float32)),
        [
            pltpu.VMEM(forward_rows.shape[1:], half),
            pltpu.VMEM(backward_rows.shape[1:], half),
            pltpu.VMEM(norm_gain.shape, jnp.float32),
            pltpu.VMEM(router_weight.shape[1:], jnp.float32),
            pltpu.SemaphoreType.DMA((4,)),
        ],
        0,
        me,
        *(
            pltpu.with_memory_space_constraint(a, pltpu.HBM)
            for a in (forward_rows[0], backward_rows[0], norm_gain, router_weight[0])
        ),
        scalars=1,
        space=pltpu.HBM,
    )
    packed_in = w_gate_up[0]
    chosen = route_ids[:, :, 0].transpose(0, 1, 3, 2)
    down_t = w_down[0].T
    for moment in range(steps_total):
        rows = gathered(copies)
        (hidden,) = local(
            lambda *refs: hidden_kernel(sizes, moment, sharers, *refs),
            (jax.ShapeDtypeStruct((sizes[1], 32, LANES), half),),
            [pltpu.VMEM((width, LANES), half)],
            2 * width * columns * LANES,
            me,
            rows,
            packed_in,
            chosen,
            scalars=1,
        )
        units = gathered(hidden)
        scratch = [pltpu.VMEM((all_units, LANES), half)]
        flops = 2 * all_units * share * LANES
        if moment + 1 < steps_total:
            (raw,) = local(
                lambda *refs: middle_kernel(sizes, *refs),
                (jax.ShapeDtypeStruct(tile, half),),
                scratch,
                flops,
                units,
                down_t,
                state,
            )
            copies, state = local(
                pass_kernel,
                entry_outs,
                [],
                0,
                passed_along(raw, "pipe", 1),
                passed_along(raw, "pipe", -1),
                coefs,
            )
        else:
            rows_out = jax.ShapeDtypeStruct((forward_rows.shape[1], share), half)
            outs = local(
                lambda *refs: last_kernel(sizes, *refs),
                (rows_out, rows_out),
                scratch,
                flops,
                units,
                down_t,
                state,
            )
    return (outs[0][None], outs[1][None])


def solution(mesh):
    fine = Mesh(mesh.devices.reshape(-1, 4, 4, 4), ("pipe", *EXPERT))
    return jax.shard_map(
        shards,
        mesh=fine,
        in_specs=(
            P("pipe", None, EXPERT),
            P("pipe", None, EXPERT),
            P(None, None, "pipe", None, None),
            P("pipe", None),
            P("pipe", None, None),
            P("pipe", None, EXPERT),
            P("pipe", None, EXPERT),
        ),
        out_specs=(P("pipe", None, EXPERT), P("pipe", None, EXPERT)),
        check_vma=False,
    )
```

```python
import jax
import jax.numpy as jnp
from jax import lax
from jax.experimental import pallas as pl
from jax.experimental.pallas import tpu as pltpu
from jax.sharding import Mesh, PartitionSpec as P

EPSILON = 1e-06
ROUTE_SCALE = 2.5
PLANE = ("y", "x")
ROW = ("zh", "x")
EXPERT = ("y", "zh", "x")
LANES = 128
STATS = 16


def passed_along(block, axis, distance):
    devices = range(lax.axis_size(axis))
    route = [(i - distance, i) for i in devices if i - distance in devices]
    return lax.ppermute(block, axis, route)


def everyone(copies, axes):
    return lax.all_to_all(copies, axes, 0, 0)


def spread(block, axes):
    size = lax.axis_size(axes)
    return everyone(jnp.broadcast_to(block[None], (size, *block.shape)), axes)


def gathered_rows(copies, by_gather):
    row = everyone(copies, ROW)
    full = lax.all_gather(row, "y") if by_gather else spread(row, "y")
    return full.reshape(-1, *copies.shape[1:])


def gathered_units(copies):
    full = spread(everyone(copies, "zh"), PLANE)
    return full.reshape(-1, *copies.shape[1:])


def lower_lanes(shape):
    return lax.broadcasted_iota(jnp.int32, shape, 1) < LANES // 2


def turned(value):
    return pltpu.roll(value, LANES // 2, 1)


def natural(place, sizes):
    y, zh, x = sizes
    at_y, rest = divmod(place, x * zh)
    at_x, at_zh = divmod(rest, zh)
    return (at_y * zh + at_zh) * x + at_x


def write_tile(rows, coefs, tile_ref):
    scaled = rows * coefs[:, 0:1]
    sums = [jnp.sum(rows * rows, axis=0, keepdims=True)]
    for e in range(1, 5):
        sums.append(jnp.sum(rows * coefs[:, e : e + 1], axis=0, keepdims=True))
    sums.append(jnp.zeros((3, LANES), jnp.float32))
    sums = jnp.concatenate(sums, axis=0)
    high = sums.astype(jnp.bfloat16).astype(jnp.float32)
    upper = jnp.concatenate([scaled[64:], high, sums - high], axis=0)
    tile = jnp.where(lower_lanes((64, LANES)), scaled[:64], turned(upper))
    tile = tile.astype(jnp.bfloat16)
    for copy in range(tile_ref.shape[0]):
        tile_ref[copy] = tile


def enter_kernel(
    me_ref,
    forward_hbm,
    backward_hbm,
    gain_hbm,
    router_hbm,
    tile_ref,
    state_ref,
    coefs_ref,
    forward_ref,
    backward_ref,
    gain_ref,
    router_ref,
    arrived,
):
    pairs = (
        (gain_hbm, gain_ref),
        (router_hbm, router_ref),
        (forward_hbm, forward_ref),
        (backward_hbm, backward_ref),
    )
    fetches = [
        pltpu.make_async_copy(source, target, arrived.at[i])
        for i, (source, target) in enumerate(pairs)
    ]
    for fetch in fetches:
        fetch.start()
    for fetch in fetches:
        fetch.wait()
    share = forward_ref.shape[1]
    window = 2 * LANES
    start = me_ref[0] * share
    last = gain_ref.shape[1] // LANES - 2
    base = pl.multiple_of(jnp.minimum(start // LANES, last) * LANES, LANES)
    gain = gain_ref[:, pl.ds(base, window)]
    router = router_ref[:, pl.ds(base, window)]
    coefs = jnp.concatenate(
        [gain, router * gain, jnp.zeros((3, window), jnp.float32)], axis=0
    )
    coefs = pltpu.roll(coefs, lax.rem(window - (start - base), window), 1)
    coefs = coefs[:, :LANES].T[:share]
    coefs_ref[...] = coefs
    f = forward_ref[...].astype(jnp.float32)
    b = backward_ref[...].astype(jnp.float32)
    rows = jnp.concatenate([f, b, f, b], axis=0).T
    state_ref[...] = rows
    write_tile(rows, coefs, tile_ref)


def pass_kernel(previous_ref, next_ref, coefs_ref, tile_ref, state_ref):
    lane = lax.broadcasted_iota(jnp.int32, (64, LANES), 1)
    mixed = jnp.where(
        lane % 64 < 32,
        previous_ref[...].astype(jnp.float32),
        next_ref[...].astype(jnp.float32),
    )
    rows = jnp.concatenate([mixed, turned(mixed)[:48]], axis=0)
    state_ref[...] = rows
    write_tile(rows, coefs_ref[...], tile_ref)


def hidden_kernel(
    moment, sharers, me_ref, gathered_ref, weight_ref, ids_ref, out_ref, rows_ref
):
    width = weight_ref.shape[0]
    share = weight_ref.shape[0] // gathered_ref.shape[0]
    stats = jnp.zeros((STATS, LANES), jnp.float32)
    for place in range(gathered_ref.shape[0]):
        tile = gathered_ref[place].astype(jnp.float32)
        start = place * share
        rows_ref[start : start + 64, :] = gathered_ref[place]
        rows_ref[start + 64 : start + share, :] = turned(tile[:48]).astype(jnp.bfloat16)
        stats = stats + tile[48:]
    stats = turned(stats[:8] + stats[8:])
    inverse = lax.rsqrt(stats[0:1] / width + EPSILON)
    projected = lax.dot_general(
        weight_ref[...],
        rows_ref[...],
        (((0,), (0,)), ((), ())),
        preferred_element_type=jnp.float32,
    ) * inverse
    scores = 1.0 / (1.0 + jnp.exp(-(stats[1:5] * inverse)))
    own = lax.div(me_ref[0], sharers)
    chosen = jnp.concatenate([ids_ref[moment, 0], ids_ref[moment, 1]] * 2, axis=1)
    total = jnp.zeros((1, LANES), jnp.float32)
    mine = jnp.zeros((1, LANES), jnp.float32)
    for k in range(chosen.shape[0]):
        ids = chosen[k : k + 1]
        picked = jnp.zeros((1, LANES), jnp.float32)
        for e in range(4):
            picked = jnp.where(ids == e, scores[e : e + 1], picked)
        total = total + picked
        mine = mine + jnp.where(ids == own, picked, 0.0)
    weight = ROUTE_SCALE * (mine / total)
    gate, up = projected[:64], projected[64:]
    hidden = gate / (1.0 + jnp.exp(-gate)) * up * weight
    folded = jnp.where(lower_lanes((32, LANES)), hidden[:32], turned(hidden[32:]))
    folded = folded.astype(jnp.bfloat16)
    for copy in range(out_ref.shape[0]):
        out_ref[copy] = folded


def updated(sizes, gathered_ref, weight_ref, state_ref, rows_ref):
    for place in range(gathered_ref.shape[0]):
        start = natural(place, sizes) * 64
        rows_ref[start : start + 32, :] = gathered_ref[place]
        rows_ref[start + 32 : start + 64, :] = turned(
            gathered_ref[place].astype(jnp.float32)
        ).astype(jnp.bfloat16)
    return state_ref[...] + jnp.dot(
        weight_ref[...], rows_ref[...], preferred_element_type=jnp.float32
    )


def middle_kernel(sizes, gathered_ref, weight_ref, state_ref, out_ref, rows_ref):
    state = updated(sizes, gathered_ref, weight_ref, state_ref, rows_ref)
    upper = jnp.concatenate([state[64:], jnp.zeros((16, LANES), jnp.float32)], axis=0)
    tile = jnp.where(lower_lanes((64, LANES)), state[:64], turned(upper))
    out_ref[...] = tile.astype(jnp.bfloat16)


def last_kernel(sizes, gathered_ref, weight_ref, state_ref, forward_ref, backward_ref, rows_ref):
    state = updated(sizes, gathered_ref, weight_ref, state_ref, rows_ref).T
    forward_ref[...] = state[:32].astype(jnp.bfloat16)
    backward_ref[...] = state[32:64].astype(jnp.bfloat16)


def local(kernel, outs, scratch, flops, *args, scalars=0, space=pltpu.VMEM, vmem=16):
    onchip = pl.BlockSpec(memory_space=pltpu.VMEM)
    given = pl.BlockSpec(memory_space=space)
    smem = pl.BlockSpec(memory_space=pltpu.SMEM)
    moved = sum(a.size * a.dtype.itemsize for a in (*args, *outs))
    return pl.pallas_call(
        kernel,
        out_shape=outs,
        in_specs=[smem] * scalars + [given] * (len(args) - scalars),
        out_specs=tuple(onchip for _ in outs),
        scratch_shapes=scratch,
        cost_estimate=pl.CostEstimate(flops=flops, bytes_accessed=moved, transcendentals=0),
        compiler_params=pltpu.CompilerParams(vmem_limit_bytes=vmem * 2**20),
    )(*args)


def shards(forward_rows, backward_rows, route_ids, norm_gain, router_weight, w_gate_up, w_down):
    sizes = tuple(lax.axis_size(a) for a in EXPERT)
    share = forward_rows.shape[2]
    width, columns = w_gate_up.shape[1:]
    all_units = w_down.shape[1]
    me = lax.axis_index(EXPERT).reshape(1)
    sharers = all_units // router_weight.shape[1] // (columns // 2)
    steps_total = route_ids.shape[0]
    tile = (64, LANES)
    half = jnp.bfloat16

    entry_outs = (
        jax.ShapeDtypeStruct((sizes[1] * sizes[2], *tile), half),
        jax.ShapeDtypeStruct((share, LANES), jnp.float32),
    )
    copies, state, coefs = local(
        enter_kernel,
        (*entry_outs, jax.ShapeDtypeStruct((share, 8), jnp.float32)),
        [
            pltpu.VMEM(forward_rows.shape[1:], half),
            pltpu.VMEM(backward_rows.shape[1:], half),
            pltpu.VMEM(norm_gain.shape, jnp.float32),
            pltpu.VMEM(router_weight.shape[1:], jnp.float32),
            pltpu.SemaphoreType.DMA((4,)),
        ],
        0,
        me,
        *(
            pltpu.with_memory_space_constraint(a, pltpu.HBM)
            for a in (forward_rows[0], backward_rows[0], norm_gain, router_weight[0])
        ),
        scalars=1,
        space=pltpu.HBM,
    )
    packed_in = w_gate_up[0]
    chosen = route_ids[:, :, 0].transpose(0, 1, 3, 2)
    down_t = w_down[0].T
    for moment in range(steps_total):
        rows = gathered_rows(copies, moment == 0)
        (hidden,) = local(
            lambda *refs: hidden_kernel(moment, sharers, *refs),
            (jax.ShapeDtypeStruct((sizes[1], 32, LANES), half),),
            [pltpu.VMEM((width, LANES), half)],
            2 * width * columns * LANES,
            me,
            rows,
            packed_in,
            chosen,
            scalars=1,
        )
        units = gathered_units(hidden)
        scratch = [pltpu.VMEM((all_units, LANES), half)]
        flops = 2 * all_units * share * LANES
        if moment + 1 < steps_total:
            (raw,) = local(
                lambda *refs: middle_kernel(sizes, *refs),
                (jax.ShapeDtypeStruct(tile, half),),
                scratch,
                flops,
                units,
                down_t,
                state,
            )
            copies, state = local(
                pass_kernel,
                entry_outs,
                [],
                0,
                passed_along(raw, "pipe", 1),
                passed_along(raw, "pipe", -1),
                coefs,
            )
        else:
            rows_out = jax.ShapeDtypeStruct((forward_rows.shape[1], share), half)
            outs = local(
                lambda *refs: last_kernel(sizes, *refs),
                (rows_out, rows_out),
                scratch,
                flops,
                units,
                down_t,
                state,
            )
    return (outs[0][None], outs[1][None])


def solution(mesh):
    fine = Mesh(mesh.devices.reshape(-1, 4, 4, 4), ("pipe", *EXPERT))
    return jax.shard_map(
        shards,
        mesh=fine,
        in_specs=(
            P("pipe", None, EXPERT),
            P("pipe", None, EXPERT),
            P(None, None, "pipe", None, None),
            P("pipe", None),
            P("pipe", None, None),
            P("pipe", None, EXPERT),
            P("pipe", None, EXPERT),
        ),
        out_specs=(P("pipe", None, EXPERT), P("pipe", None, EXPERT)),
        check_vma=False,
    )
```

```python
import jax
import jax.numpy as jnp
from jax import lax
from jax.experimental import pallas as pl
from jax.experimental.pallas import tpu as pltpu
from jax.sharding import Mesh, PartitionSpec as P

EPSILON = 1e-06
ROUTE_SCALE = 2.5
PLANE = ("y", "x")
EXPERT = ("y", "zh", "x")
LANES = 128
STATS = 16


def passed_along(block, axis, distance):
    devices = range(lax.axis_size(axis))
    route = [(i - distance, i) for i in devices if i - distance in devices]
    return lax.ppermute(block, axis, route)


def gathered(tile):
    column = lax.all_gather(tile, "zh")
    copies = jnp.broadcast_to(column[None], (lax.axis_size(PLANE), *column.shape))
    return lax.all_to_all(copies, PLANE, 0, 0).reshape(-1, *tile.shape)


def lower_lanes(shape):
    return lax.broadcasted_iota(jnp.int32, shape, 1) < LANES // 2


def turned(value):
    return pltpu.roll(value, LANES // 2, 1)


def natural(place, sizes):
    y, zh, x = sizes
    at_y, rest = divmod(place, x * zh)
    at_x, at_zh = divmod(rest, zh)
    return (at_y * zh + at_zh) * x + at_x


def write_tile(rows, coefs, tile_ref):
    scaled = rows * coefs[:, 0:1]
    sums = [jnp.sum(rows * rows, axis=0, keepdims=True)]
    for e in range(1, 5):
        sums.append(jnp.sum(rows * coefs[:, e : e + 1], axis=0, keepdims=True))
    sums.append(jnp.zeros((3, LANES), jnp.float32))
    sums = jnp.concatenate(sums, axis=0)
    high = sums.astype(jnp.bfloat16).astype(jnp.float32)
    upper = jnp.concatenate([scaled[64:], high, sums - high], axis=0)
    tile = jnp.where(lower_lanes((64, LANES)), scaled[:64], turned(upper))
    tile = tile.astype(jnp.bfloat16)
    tile_ref[...] = tile


def enter_kernel(
    me_ref,
    forward_hbm,
    backward_hbm,
    gain_hbm,
    router_hbm,
    tile_ref,
    state_ref,
    coefs_ref,
    forward_ref,
    backward_ref,
    gain_ref,
    router_ref,
    arrived,
):
    pairs = (
        (gain_hbm, gain_ref),
        (router_hbm, router_ref),
        (forward_hbm, forward_ref),
        (backward_hbm, backward_ref),
    )
    fetches = [
        pltpu.make_async_copy(source, target, arrived.at[i])
        for i, (source, target) in enumerate(pairs)
    ]
    for fetch in fetches:
        fetch.start()
    for fetch in fetches:
        fetch.wait()
    share = forward_ref.shape[1]
    window = 2 * LANES
    start = me_ref[0] * share
    last = gain_ref.shape[1] // LANES - 2
    base = pl.multiple_of(jnp.minimum(start // LANES, last) * LANES, LANES)
    gain = gain_ref[:, pl.ds(base, window)]
    router = router_ref[:, pl.ds(base, window)]
    coefs = jnp.concatenate(
        [gain, router * gain, jnp.zeros((3, window), jnp.float32)], axis=0
    )
    coefs = pltpu.roll(coefs, lax.rem(window - (start - base), window), 1)
    coefs = coefs[:, :LANES].T[:share]
    coefs_ref[...] = coefs
    f = forward_ref[...].astype(jnp.float32)
    b = backward_ref[...].astype(jnp.float32)
    rows = jnp.concatenate([f, b, f, b], axis=0).T
    state_ref[...] = rows
    write_tile(rows, coefs, tile_ref)


def pass_kernel(previous_ref, next_ref, coefs_ref, tile_ref, state_ref):
    lane = lax.broadcasted_iota(jnp.int32, (64, LANES), 1)
    mixed = jnp.where(
        lane % 64 < 32,
        previous_ref[...].astype(jnp.float32),
        next_ref[...].astype(jnp.float32),
    )
    rows = jnp.concatenate([mixed, turned(mixed)[:48]], axis=0)
    state_ref[...] = rows
    write_tile(rows, coefs_ref[...], tile_ref)


def hidden_kernel(
    sizes, moment, sharers, me_ref, gathered_ref, weight_ref, ids_ref, out_ref, rows_ref
):
    width = weight_ref.shape[0]
    share = weight_ref.shape[0] // gathered_ref.shape[0]
    stats = jnp.zeros((STATS, LANES), jnp.float32)
    for place in range(gathered_ref.shape[0]):
        tile = gathered_ref[place].astype(jnp.float32)
        start = natural(place, sizes) * share
        rows_ref[start : start + 64, :] = gathered_ref[place]
        rows_ref[start + 64 : start + share, :] = turned(tile[:48]).astype(jnp.bfloat16)
        stats = stats + tile[48:]
    stats = turned(stats[:8] + stats[8:])
    inverse = lax.rsqrt(stats[0:1] / width + EPSILON)
    projected = lax.dot_general(
        weight_ref[...],
        rows_ref[...],
        (((0,), (0,)), ((), ())),
        preferred_element_type=jnp.float32,
    ) * inverse
    scores = 1.0 / (1.0 + jnp.exp(-(stats[1:5] * inverse)))
    own = lax.div(me_ref[0], sharers)
    chosen = jnp.concatenate([ids_ref[moment, 0], ids_ref[moment, 1]] * 2, axis=1)
    total = jnp.zeros((1, LANES), jnp.float32)
    mine = jnp.zeros((1, LANES), jnp.float32)
    for k in range(chosen.shape[0]):
        ids = chosen[k : k + 1]
        picked = jnp.zeros((1, LANES), jnp.float32)
        for e in range(4):
            picked = jnp.where(ids == e, scores[e : e + 1], picked)
        total = total + picked
        mine = mine + jnp.where(ids == own, picked, 0.0)
    weight = ROUTE_SCALE * (mine / total)
    gate, up = projected[:64], projected[64:]
    hidden = gate / (1.0 + jnp.exp(-gate)) * up * weight
    folded = jnp.where(lower_lanes((32, LANES)), hidden[:32], turned(hidden[32:]))
    folded = folded.astype(jnp.bfloat16)
    out_ref[...] = folded


def updated(sizes, gathered_ref, weight_ref, state_ref, rows_ref):
    for place in range(gathered_ref.shape[0]):
        start = natural(place, sizes) * 64
        rows_ref[start : start + 32, :] = gathered_ref[place]
        rows_ref[start + 32 : start + 64, :] = turned(
            gathered_ref[place].astype(jnp.float32)
        ).astype(jnp.bfloat16)
    return state_ref[...] + jnp.dot(
        weight_ref[...], rows_ref[...], preferred_element_type=jnp.float32
    )


def middle_kernel(sizes, gathered_ref, weight_ref, state_ref, out_ref, rows_ref):
    state = updated(sizes, gathered_ref, weight_ref, state_ref, rows_ref)
    upper = jnp.concatenate([state[64:], jnp.zeros((16, LANES), jnp.float32)], axis=0)
    tile = jnp.where(lower_lanes((64, LANES)), state[:64], turned(upper))
    out_ref[...] = tile.astype(jnp.bfloat16)


def last_kernel(sizes, gathered_ref, weight_ref, state_ref, forward_ref, backward_ref, rows_ref):
    state = updated(sizes, gathered_ref, weight_ref, state_ref, rows_ref).T
    forward_ref[...] = state[:32].astype(jnp.bfloat16)
    backward_ref[...] = state[32:64].astype(jnp.bfloat16)


def local(kernel, outs, scratch, flops, *args, scalars=0, space=pltpu.VMEM, vmem=16):
    onchip = pl.BlockSpec(memory_space=pltpu.VMEM)
    given = pl.BlockSpec(memory_space=space)
    smem = pl.BlockSpec(memory_space=pltpu.SMEM)
    moved = sum(a.size * a.dtype.itemsize for a in (*args, *outs))
    return pl.pallas_call(
        kernel,
        out_shape=outs,
        in_specs=[smem] * scalars + [given] * (len(args) - scalars),
        out_specs=tuple(onchip for _ in outs),
        scratch_shapes=scratch,
        cost_estimate=pl.CostEstimate(flops=flops, bytes_accessed=moved, transcendentals=0),
        compiler_params=pltpu.CompilerParams(vmem_limit_bytes=vmem * 2**20),
    )(*args)


def shards(forward_rows, backward_rows, route_ids, norm_gain, router_weight, w_gate_up, w_down):
    sizes = tuple(lax.axis_size(a) for a in EXPERT)
    share = forward_rows.shape[2]
    width, columns = w_gate_up.shape[1:]
    all_units = w_down.shape[1]
    me = lax.axis_index(EXPERT).reshape(1)
    sharers = all_units // router_weight.shape[1] // (columns // 2)
    steps_total = route_ids.shape[0]
    tile = (64, LANES)
    half = jnp.bfloat16

    entry_outs = (
        jax.ShapeDtypeStruct(tile, half),
        jax.ShapeDtypeStruct((share, LANES), jnp.float32),
    )
    sent, state, coefs = local(
        enter_kernel,
        (*entry_outs, jax.ShapeDtypeStruct((share, 8), jnp.float32)),
        [
            pltpu.VMEM(forward_rows.shape[1:], half),
            pltpu.VMEM(backward_rows.shape[1:], half),
            pltpu.VMEM(norm_gain.shape, jnp.float32),
            pltpu.VMEM(router_weight.shape[1:], jnp.float32),
            pltpu.SemaphoreType.DMA((4,)),
        ],
        0,
        me,
        *(
            pltpu.with_memory_space_constraint(a, pltpu.HBM)
            for a in (forward_rows[0], backward_rows[0], norm_gain, router_weight[0])
        ),
        scalars=1,
        space=pltpu.HBM,
    )
    packed_in = w_gate_up[0]
    chosen = route_ids[:, :, 0].transpose(0, 1, 3, 2)
    down_t = w_down[0].T
    for moment in range(steps_total):
        rows = gathered(sent)
        (hidden,) = local(
            lambda *refs: hidden_kernel(sizes, moment, sharers, *refs),
            (jax.ShapeDtypeStruct((32, LANES), half),),
            [pltpu.VMEM((width, LANES), half)],
            2 * width * columns * LANES,
            me,
            rows,
            packed_in,
            chosen,
            scalars=1,
        )
        units = gathered(hidden)
        scratch = [pltpu.VMEM((all_units, LANES), half)]
        flops = 2 * all_units * share * LANES
        if moment + 1 < steps_total:
            (raw,) = local(
                lambda *refs: middle_kernel(sizes, *refs),
                (jax.ShapeDtypeStruct(tile, half),),
                scratch,
                flops,
                units,
                down_t,
                state,
            )
            sent, state = local(
                pass_kernel,
                entry_outs,
                [],
                0,
                passed_along(raw, "pipe", 1),
                passed_along(raw, "pipe", -1),
                coefs,
            )
        else:
            rows_out = jax.ShapeDtypeStruct((forward_rows.shape[1], share), half)
            outs = local(
                lambda *refs: last_kernel(sizes, *refs),
                (rows_out, rows_out),
                scratch,
                flops,
                units,
                down_t,
                state,
            )
    return (outs[0][None], outs[1][None])


def solution(mesh):
    fine = Mesh(mesh.devices.reshape(-1, 4, 4, 4), ("pipe", *EXPERT))
    return jax.shard_map(
        shards,
        mesh=fine,
        in_specs=(
            P("pipe", None, EXPERT),
            P("pipe", None, EXPERT),
            P(None, None, "pipe", None, None),
            P("pipe", None),
            P("pipe", None, None),
            P("pipe", None, EXPERT),
            P("pipe", None, EXPERT),
        ),
        out_specs=(P("pipe", None, EXPERT), P("pipe", None, EXPERT)),
        check_vma=False,
    )
```

```python
import jax
import jax.numpy as jnp
from jax import lax
from jax.experimental import pallas as pl
from jax.experimental.pallas import tpu as pltpu
from jax.sharding import Mesh, PartitionSpec as P

EPSILON = 1e-06
ROUTE_SCALE = 2.5
PLANE = ("y", "x")
EXPERT = ("y", "zh", "x")
LANES = 128
STATS = 16


def passed_along(block, axis, distance):
    devices = range(lax.axis_size(axis))
    route = [(i - distance, i) for i in devices if i - distance in devices]
    return lax.ppermute(block, axis, route)


def gathered(tile):
    column = lax.all_gather(tile, "zh")
    copies = jnp.broadcast_to(column[None], (lax.axis_size(PLANE), *column.shape))
    return lax.all_to_all(copies, PLANE, 0, 0).reshape(-1, *tile.shape)


def lower_lanes(shape):
    return lax.broadcasted_iota(jnp.int32, shape, 1) < LANES // 2


def turned(value):
    return pltpu.roll(value, LANES // 2, 1)


def exchanged(value):
    half = LANES // 2
    return jnp.concatenate([value[:, half:], value[:, :half]], axis=1)


def natural(place, sizes):
    y, zh, x = sizes
    at_y, rest = divmod(place, x * zh)
    at_x, at_zh = divmod(rest, zh)
    return (at_y * zh + at_zh) * x + at_x


def write_tile(rows, coefs, tile_ref):
    scaled = rows * coefs[:, 0:1]
    sums = [jnp.sum(rows * rows, axis=0, keepdims=True)]
    for e in range(1, 5):
        sums.append(jnp.sum(rows * coefs[:, e : e + 1], axis=0, keepdims=True))
    sums.append(jnp.zeros((3, LANES), jnp.float32))
    sums = jnp.concatenate(sums, axis=0)
    high = sums.astype(jnp.bfloat16).astype(jnp.float32)
    upper = jnp.concatenate([scaled[64:], high, sums - high], axis=0)
    tile = jnp.where(lower_lanes((64, LANES)), scaled[:64], turned(upper))
    tile = tile.astype(jnp.bfloat16)
    tile_ref[...] = tile


def enter_kernel(
    me_ref,
    forward_hbm,
    backward_hbm,
    gain_hbm,
    router_hbm,
    tile_ref,
    state_ref,
    coefs_ref,
    forward_ref,
    backward_ref,
    gain_ref,
    router_ref,
    arrived,
):
    pairs = (
        (gain_hbm, gain_ref),
        (router_hbm, router_ref),
        (forward_hbm, forward_ref),
        (backward_hbm, backward_ref),
    )
    fetches = [
        pltpu.make_async_copy(source, target, arrived.at[i])
        for i, (source, target) in enumerate(pairs)
    ]
    for fetch in fetches:
        fetch.start()
    for fetch in fetches:
        fetch.wait()
    share = forward_ref.shape[1]
    window = 2 * LANES
    start = me_ref[0] * share
    last = gain_ref.shape[1] // LANES - 2
    base = pl.multiple_of(jnp.minimum(start // LANES, last) * LANES, LANES)
    gain = gain_ref[:, pl.ds(base, window)]
    router = router_ref[:, pl.ds(base, window)]
    coefs = jnp.concatenate(
        [gain, router * gain, jnp.zeros((3, window), jnp.float32)], axis=0
    )
    coefs = pltpu.roll(coefs, lax.rem(window - (start - base), window), 1)
    coefs = coefs[:, :LANES].T[:share]
    coefs_ref[...] = coefs
    f = forward_ref[...].astype(jnp.float32)
    b = backward_ref[...].astype(jnp.float32)
    rows = jnp.concatenate([f, b, f, b], axis=0).T
    state_ref[...] = rows
    write_tile(rows, coefs, tile_ref)


def pass_kernel(previous_ref, next_ref, coefs_ref, tile_ref, state_ref):
    lane = lax.broadcasted_iota(jnp.int32, (64, LANES), 1)
    mixed = jnp.where(
        lane % 64 < 32,
        previous_ref[...].astype(jnp.float32),
        next_ref[...].astype(jnp.float32),
    )
    rows = jnp.concatenate([mixed, turned(mixed)[:48]], axis=0)
    state_ref[...] = rows
    write_tile(rows, coefs_ref[...], tile_ref)


def hidden_kernel(
    sizes, moment, sharers, me_ref, gathered_ref, weight_ref, ids_ref, out_ref, rows_ref
):
    width = weight_ref.shape[0]
    share = weight_ref.shape[0] // gathered_ref.shape[0]
    stats = jnp.zeros((STATS, LANES), jnp.float32)
    for place in range(gathered_ref.shape[0]):
        start = natural(place, sizes) * share
        rows_ref[start : start + 64, :] = gathered_ref[place]
        rows_ref[start + 64 : start + share, :] = exchanged(gathered_ref[place, :48])
        stats = stats + gathered_ref[place, 48:].astype(jnp.float32)
    stats = turned(stats[:8] + stats[8:])
    inverse = lax.rsqrt(stats[0:1] / width + EPSILON)
    projected = lax.dot_general(
        weight_ref[...],
        rows_ref[...],
        (((0,), (0,)), ((), ())),
        preferred_element_type=jnp.float32,
    ) * inverse
    scores = 1.0 / (1.0 + jnp.exp(-(stats[1:5] * inverse)))
    own = lax.div(me_ref[0], sharers)
    chosen = jnp.concatenate([ids_ref[moment, 0], ids_ref[moment, 1]] * 2, axis=1)
    total = jnp.zeros((1, LANES), jnp.float32)
    mine = jnp.zeros((1, LANES), jnp.float32)
    for k in range(chosen.shape[0]):
        ids = chosen[k : k + 1]
        picked = jnp.zeros((1, LANES), jnp.float32)
        for e in range(4):
            picked = jnp.where(ids == e, scores[e : e + 1], picked)
        total = total + picked
        mine = mine + jnp.where(ids == own, picked, 0.0)
    weight = ROUTE_SCALE * (mine / total)
    gate, up = projected[:64], projected[64:]
    hidden = gate / (1.0 + jnp.exp(-gate)) * up * weight
    folded = jnp.where(lower_lanes((32, LANES)), hidden[:32], turned(hidden[32:]))
    folded = folded.astype(jnp.bfloat16)
    out_ref[...] = folded


def updated(sizes, gathered_ref, weight_ref, state_ref, rows_ref):
    for place in range(gathered_ref.shape[0]):
        start = natural(place, sizes) * 64
        rows_ref[start : start + 32, :] = gathered_ref[place]
        rows_ref[start + 32 : start + 64, :] = exchanged(gathered_ref[place])
    return state_ref[...] + jnp.dot(
        weight_ref[...], rows_ref[...], preferred_element_type=jnp.float32
    )


def middle_kernel(sizes, gathered_ref, weight_ref, state_ref, out_ref, rows_ref):
    state = updated(sizes, gathered_ref, weight_ref, state_ref, rows_ref)
    upper = jnp.concatenate([state[64:], jnp.zeros((16, LANES), jnp.float32)], axis=0)
    tile = jnp.where(lower_lanes((64, LANES)), state[:64], turned(upper))
    out_ref[...] = tile.astype(jnp.bfloat16)


def last_kernel(sizes, gathered_ref, weight_ref, state_ref, forward_ref, backward_ref, rows_ref):
    state = updated(sizes, gathered_ref, weight_ref, state_ref, rows_ref).T
    forward_ref[...] = state[:32].astype(jnp.bfloat16)
    backward_ref[...] = state[32:64].astype(jnp.bfloat16)


def local(kernel, outs, scratch, flops, *args, scalars=0, space=pltpu.VMEM, vmem=16):
    onchip = pl.BlockSpec(memory_space=pltpu.VMEM)
    given = pl.BlockSpec(memory_space=space)
    smem = pl.BlockSpec(memory_space=pltpu.SMEM)
    moved = sum(a.size * a.dtype.itemsize for a in (*args, *outs))
    return pl.pallas_call(
        kernel,
        out_shape=outs,
        in_specs=[smem] * scalars + [given] * (len(args) - scalars),
        out_specs=tuple(onchip for _ in outs),
        scratch_shapes=scratch,
        cost_estimate=pl.CostEstimate(flops=flops, bytes_accessed=moved, transcendentals=0),
        compiler_params=pltpu.CompilerParams(vmem_limit_bytes=vmem * 2**20),
    )(*args)


def shards(forward_rows, backward_rows, route_ids, norm_gain, router_weight, w_gate_up, w_down):
    sizes = tuple(lax.axis_size(a) for a in EXPERT)
    share = forward_rows.shape[2]
    width, columns = w_gate_up.shape[1:]
    all_units = w_down.shape[1]
    me = lax.axis_index(EXPERT).reshape(1)
    sharers = all_units // router_weight.shape[1] // (columns // 2)
    steps_total = route_ids.shape[0]
    tile = (64, LANES)
    half = jnp.bfloat16

    entry_outs = (
        jax.ShapeDtypeStruct(tile, half),
        jax.ShapeDtypeStruct((share, LANES), jnp.float32),
    )
    sent, state, coefs = local(
        enter_kernel,
        (*entry_outs, jax.ShapeDtypeStruct((share, 8), jnp.float32)),
        [
            pltpu.VMEM(forward_rows.shape[1:], half),
            pltpu.VMEM(backward_rows.shape[1:], half),
            pltpu.VMEM(norm_gain.shape, jnp.float32),
            pltpu.VMEM(router_weight.shape[1:], jnp.float32),
            pltpu.SemaphoreType.DMA((4,)),
        ],
        0,
        me,
        *(
            pltpu.with_memory_space_constraint(a, pltpu.HBM)
            for a in (forward_rows[0], backward_rows[0], norm_gain, router_weight[0])
        ),
        scalars=1,
        space=pltpu.HBM,
    )
    packed_in = w_gate_up[0]
    chosen = route_ids[:, :, 0].transpose(0, 1, 3, 2)
    down_t = w_down[0].T
    for moment in range(steps_total):
        rows = gathered(sent)
        (hidden,) = local(
            lambda *refs: hidden_kernel(sizes, moment, sharers, *refs),
            (jax.ShapeDtypeStruct((32, LANES), half),),
            [pltpu.VMEM((width, LANES), half)],
            2 * width * columns * LANES,
            me,
            rows,
            packed_in,
            chosen,
            scalars=1,
        )
        units = gathered(hidden)
        scratch = [pltpu.VMEM((all_units, LANES), half)]
        flops = 2 * all_units * share * LANES
        if moment + 1 < steps_total:
            (raw,) = local(
                lambda *refs: middle_kernel(sizes, *refs),
                (jax.ShapeDtypeStruct(tile, half),),
                scratch,
                flops,
                units,
                down_t,
                state,
            )
            sent, state = local(
                pass_kernel,
                entry_outs,
                [],
                0,
                passed_along(raw, "pipe", 1),
                passed_along(raw, "pipe", -1),
                coefs,
            )
        else:
            rows_out = jax.ShapeDtypeStruct((forward_rows.shape[1], share), half)
            outs = local(
                lambda *refs: last_kernel(sizes, *refs),
                (rows_out, rows_out),
                scratch,
                flops,
                units,
                down_t,
                state,
            )
    return (outs[0][None], outs[1][None])


def solution(mesh):
    fine = Mesh(mesh.devices.reshape(-1, 4, 4, 4), ("pipe", *EXPERT))
    return jax.shard_map(
        shards,
        mesh=fine,
        in_specs=(
            P("pipe", None, EXPERT),
            P("pipe", None, EXPERT),
            P(None, None, "pipe", None, None),
            P("pipe", None),
            P("pipe", None, None),
            P("pipe", None, EXPERT),
            P("pipe", None, EXPERT),
        ),
        out_specs=(P("pipe", None, EXPERT), P("pipe", None, EXPERT)),
        check_vma=False,
    )
```

```python
import jax
import jax.numpy as jnp
from jax import lax
from jax.experimental import pallas as pl
from jax.experimental.pallas import tpu as pltpu
from jax.sharding import Mesh, PartitionSpec as P

EPSILON = 1e-06
ROUTE_SCALE = 2.5
PLANE = ("y", "x")
EXPERT = ("y", "zh", "x")
LANES = 128
STATS = 16


def swapped(block, axis, first):
    lower = range(first, lax.axis_size(axis) - 1, 2)
    route = [(i, i + 1) for i in lower] + [(i + 1, i) for i in lower]
    return lax.ppermute(block, axis, route)


def gathered(tile):
    column = lax.all_gather(tile, "zh")
    copies = jnp.broadcast_to(column[None], (lax.axis_size(PLANE), *column.shape))
    return lax.all_to_all(copies, PLANE, 0, 0).reshape(-1, *tile.shape)


def lower_lanes(shape):
    return lax.broadcasted_iota(jnp.int32, shape, 1) < LANES // 2


def turned(value):
    return pltpu.roll(value, LANES // 2, 1)


def exchanged(value):
    half = LANES // 2
    return jnp.concatenate([value[:, half:], value[:, :half]], axis=1)


def natural(place, sizes):
    y, zh, x = sizes
    at_y, rest = divmod(place, x * zh)
    at_x, at_zh = divmod(rest, zh)
    return (at_y * zh + at_zh) * x + at_x


def write_tile(rows, coefs, tile_ref):
    scaled = rows * coefs[:, 0:1]
    sums = [jnp.sum(rows * rows, axis=0, keepdims=True)]
    for e in range(1, 5):
        sums.append(jnp.sum(rows * coefs[:, e : e + 1], axis=0, keepdims=True))
    sums.append(jnp.zeros((3, LANES), jnp.float32))
    sums = jnp.concatenate(sums, axis=0)
    high = sums.astype(jnp.bfloat16).astype(jnp.float32)
    upper = jnp.concatenate([scaled[64:], high, sums - high], axis=0)
    tile = jnp.where(lower_lanes((64, LANES)), scaled[:64], turned(upper))
    tile = tile.astype(jnp.bfloat16)
    tile_ref[...] = tile


def enter_kernel(
    me_ref,
    forward_hbm,
    backward_hbm,
    gain_hbm,
    router_hbm,
    tile_ref,
    state_ref,
    coefs_ref,
    forward_ref,
    backward_ref,
    gain_ref,
    router_ref,
    arrived,
):
    pairs = (
        (gain_hbm, gain_ref),
        (router_hbm, router_ref),
        (forward_hbm, forward_ref),
        (backward_hbm, backward_ref),
    )
    fetches = [
        pltpu.make_async_copy(source, target, arrived.at[i])
        for i, (source, target) in enumerate(pairs)
    ]
    for fetch in fetches:
        fetch.start()
    for fetch in fetches:
        fetch.wait()
    share = forward_ref.shape[1]
    window = 2 * LANES
    start = me_ref[0] * share
    last = gain_ref.shape[1] // LANES - 2
    base = pl.multiple_of(jnp.minimum(start // LANES, last) * LANES, LANES)
    gain = gain_ref[:, pl.ds(base, window)]
    router = router_ref[:, pl.ds(base, window)]
    coefs = jnp.concatenate(
        [gain, router * gain, jnp.zeros((3, window), jnp.float32)], axis=0
    )
    coefs = pltpu.roll(coefs, lax.rem(window - (start - base), window), 1)
    coefs = coefs[:, :LANES].T[:share]
    coefs_ref[...] = coefs
    f = forward_ref[...].astype(jnp.float32)
    b = backward_ref[...].astype(jnp.float32)
    rows = jnp.concatenate([f, b, f, b], axis=0).T
    state_ref[...] = rows
    write_tile(rows, coefs, tile_ref)


def pass_kernel(section_ref, even_ref, odd_ref, coefs_ref, tile_ref, state_ref):
    lane = lax.broadcasted_iota(jnp.int32, (64, LANES), 1)
    forward = (lane % 64 < 32).astype(jnp.int32)
    mixed = jnp.where(
        forward == lax.rem(section_ref[0], 2),
        even_ref[...].astype(jnp.float32),
        odd_ref[...].astype(jnp.float32),
    )
    rows = jnp.concatenate([mixed, turned(mixed)[:48]], axis=0)
    state_ref[...] = rows
    write_tile(rows, coefs_ref[...], tile_ref)


def hidden_kernel(
    sizes, moment, sharers, me_ref, gathered_ref, weight_ref, ids_ref, out_ref, rows_ref
):
    width = weight_ref.shape[0]
    share = weight_ref.shape[0] // gathered_ref.shape[0]
    stats = jnp.zeros((STATS, LANES), jnp.float32)
    for place in range(gathered_ref.shape[0]):
        start = natural(place, sizes) * share
        rows_ref[start : start + 64, :] = gathered_ref[place]
        rows_ref[start + 64 : start + share, :] = exchanged(gathered_ref[place, :48])
        stats = stats + gathered_ref[place, 48:].astype(jnp.float32)
    stats = turned(stats[:8] + stats[8:])
    inverse = lax.rsqrt(stats[0:1] / width + EPSILON)
    projected = lax.dot_general(
        weight_ref[...],
        rows_ref[...],
        (((0,), (0,)), ((), ())),
        preferred_element_type=jnp.float32,
    ) * inverse
    scores = 1.0 / (1.0 + jnp.exp(-(stats[1:5] * inverse)))
    own = lax.div(me_ref[0], sharers)
    chosen = jnp.concatenate([ids_ref[moment, 0], ids_ref[moment, 1]] * 2, axis=1)
    total = jnp.zeros((1, LANES), jnp.float32)
    mine = jnp.zeros((1, LANES), jnp.float32)
    for k in range(chosen.shape[0]):
        ids = chosen[k : k + 1]
        picked = jnp.zeros((1, LANES), jnp.float32)
        for e in range(4):
            picked = jnp.where(ids == e, scores[e : e + 1], picked)
        total = total + picked
        mine = mine + jnp.where(ids == own, picked, 0.0)
    weight = ROUTE_SCALE * (mine / total)
    gate, up = projected[:64], projected[64:]
    hidden = gate / (1.0 + jnp.exp(-gate)) * up * weight
    folded = jnp.where(lower_lanes((32, LANES)), hidden[:32], turned(hidden[32:]))
    folded = folded.astype(jnp.bfloat16)
    out_ref[...] = folded


def updated(sizes, gathered_ref, weight_ref, state_ref, rows_ref):
    for place in range(gathered_ref.shape[0]):
        start = natural(place, sizes) * 64
        rows_ref[start : start + 32, :] = gathered_ref[place]
        rows_ref[start + 32 : start + 64, :] = exchanged(gathered_ref[place])
    return state_ref[...] + jnp.dot(
        weight_ref[...], rows_ref[...], preferred_element_type=jnp.float32
    )


def middle_kernel(sizes, gathered_ref, weight_ref, state_ref, out_ref, rows_ref):
    state = updated(sizes, gathered_ref, weight_ref, state_ref, rows_ref)
    upper = jnp.concatenate([state[64:], jnp.zeros((16, LANES), jnp.float32)], axis=0)
    tile = jnp.where(lower_lanes((64, LANES)), state[:64], turned(upper))
    out_ref[...] = tile.astype(jnp.bfloat16)


def last_kernel(sizes, gathered_ref, weight_ref, state_ref, forward_ref, backward_ref, rows_ref):
    state = updated(sizes, gathered_ref, weight_ref, state_ref, rows_ref).T
    forward_ref[...] = state[:32].astype(jnp.bfloat16)
    backward_ref[...] = state[32:64].astype(jnp.bfloat16)


def local(kernel, outs, scratch, flops, *args, scalars=0, space=pltpu.VMEM, vmem=16):
    onchip = pl.BlockSpec(memory_space=pltpu.VMEM)
    given = pl.BlockSpec(memory_space=space)
    smem = pl.BlockSpec(memory_space=pltpu.SMEM)
    moved = sum(a.size * a.dtype.itemsize for a in (*args, *outs))
    return pl.pallas_call(
        kernel,
        out_shape=outs,
        in_specs=[smem] * scalars + [given] * (len(args) - scalars),
        out_specs=tuple(onchip for _ in outs),
        scratch_shapes=scratch,
        cost_estimate=pl.CostEstimate(flops=flops, bytes_accessed=moved, transcendentals=0),
        compiler_params=pltpu.CompilerParams(vmem_limit_bytes=vmem * 2**20),
    )(*args)


def shards(forward_rows, backward_rows, route_ids, norm_gain, router_weight, w_gate_up, w_down):
    sizes = tuple(lax.axis_size(a) for a in EXPERT)
    share = forward_rows.shape[2]
    width, columns = w_gate_up.shape[1:]
    all_units = w_down.shape[1]
    me = lax.axis_index(EXPERT).reshape(1)
    sharers = all_units // router_weight.shape[1] // (columns // 2)
    steps_total = route_ids.shape[0]
    tile = (64, LANES)
    half = jnp.bfloat16

    entry_outs = (
        jax.ShapeDtypeStruct(tile, half),
        jax.ShapeDtypeStruct((share, LANES), jnp.float32),
    )
    sent, state, coefs = local(
        enter_kernel,
        (*entry_outs, jax.ShapeDtypeStruct((share, 8), jnp.float32)),
        [
            pltpu.VMEM(forward_rows.shape[1:], half),
            pltpu.VMEM(backward_rows.shape[1:], half),
            pltpu.VMEM(norm_gain.shape, jnp.float32),
            pltpu.VMEM(router_weight.shape[1:], jnp.float32),
            pltpu.SemaphoreType.DMA((4,)),
        ],
        0,
        me,
        *(
            pltpu.with_memory_space_constraint(a, pltpu.HBM)
            for a in (forward_rows[0], backward_rows[0], norm_gain, router_weight[0])
        ),
        scalars=1,
        space=pltpu.HBM,
    )
    packed_in = w_gate_up[0]
    chosen = route_ids[:, :, 0].transpose(0, 1, 3, 2)
    down_t = w_down[0].T
    for moment in range(steps_total):
        rows = gathered(sent)
        (hidden,) = local(
            lambda *refs: hidden_kernel(sizes, moment, sharers, *refs),
            (jax.ShapeDtypeStruct((32, LANES), half),),
            [pltpu.VMEM((width, LANES), half)],
            2 * width * columns * LANES,
            me,
            rows,
            packed_in,
            chosen,
            scalars=1,
        )
        units = gathered(hidden)
        scratch = [pltpu.VMEM((all_units, LANES), half)]
        flops = 2 * all_units * share * LANES
        if moment + 1 < steps_total:
            (raw,) = local(
                lambda *refs: middle_kernel(sizes, *refs),
                (jax.ShapeDtypeStruct(tile, half),),
                scratch,
                flops,
                units,
                down_t,
                state,
            )
            sent, state = local(
                pass_kernel,
                entry_outs,
                [],
                0,
                lax.axis_index("pipe").reshape(1),
                swapped(raw, "pipe", 0),
                swapped(raw, "pipe", 1),
                coefs,
                scalars=1,
            )
        else:
            rows_out = jax.ShapeDtypeStruct((forward_rows.shape[1], share), half)
            outs = local(
                lambda *refs: last_kernel(sizes, *refs),
                (rows_out, rows_out),
                scratch,
                flops,
                units,
                down_t,
                state,
            )
    return (outs[0][None], outs[1][None])


def solution(mesh):
    fine = Mesh(mesh.devices.reshape(-1, 4, 4, 4), ("pipe", *EXPERT))
    return jax.shard_map(
        shards,
        mesh=fine,
        in_specs=(
            P("pipe", None, EXPERT),
            P("pipe", None, EXPERT),
            P(None, None, "pipe", None, None),
            P("pipe", None),
            P("pipe", None, None),
            P("pipe", None, EXPERT),
            P("pipe", None, EXPERT),
        ),
        out_specs=(P("pipe", None, EXPERT), P("pipe", None, EXPERT)),
        check_vma=False,
    )
```
